32 devices in a mesh: ctx: 16 (over z, y, core), tp: 2 (over x).
Axes of the slice: x: 2, y: 2, z: 4, core: 2. Of those that a mesh axis runs over, the one named last changes fastest.
Arguments:
- query_in: bfloat16 [4096, 8192], P('ctx', 'tp'), may hold values from -6 to 6
- key_in: bfloat16 [4096, 8192], P('ctx', 'tp'), may hold values from -6 to 6
- value_in: bfloat16 [4096, 8192], P('ctx', 'tp'), may hold values from -6 to 6
- cotangent: bfloat16 [4096, 8192], P('ctx', 'tp'), may hold values from -6 to 6
- short_weight: float32 [3, 3, 8192], P(None, None, 'tp'), may hold values from -3 to 3
- long_filter: bfloat16 [4096, 8192], P('ctx', 'tp'), may hold values from -1.5 to 1.5
Outputs:
- block_out: bfloat16 [4096, 8192], P('ctx', 'tp')
- grad_query: bfloat16 [4096, 8192], P('ctx', 'tp')
- grad_key: bfloat16 [4096, 8192], P('ctx', 'tp')
- grad_value: bfloat16 [4096, 8192], P('ctx', 'tp')
- grad_short: float32 [3, 3, 8192], P(None, None, 'tp')
- grad_filter: bfloat16 [4096, 8192], P('ctx', 'tp')
The draws below stay inside these ranges and needn't reach their ends.
All inputs are finite; a program needn't handle non-finite values.
Results may differ from the reference program's by a relative error of at most 0.025.
Values may be sent and summed in bfloat16 or wider, within the bound.
A program may use at most 192 MiB of HBM per device.

```python
import math
import jax
import jax.numpy as jnp
from jax import lax

D = 8192
KS = 3
S = 128
L = 4096


def draw_cotangent(key, part):
    key = jax.random.fold_in(key, 23)
    noise_key = jax.random.fold_in(key, 0)
    position = jnp.arange(L, dtype=jnp.float32)[:, None] / L
    noise = jnp.clip(jax.random.normal(noise_key, (L, D), jnp.float32), -4.0, 4.0)
    result = noise * (0.5 + position)
    return jnp.clip(result, -6.0, 6.0).astype(jnp.bfloat16)


def draw_long_filter(key, part):
    key = jax.random.fold_in(key, 11)
    chooser, slow_key, fast_key, noise_key = jax.random.split(key, 4)
    lowest = math.log(0.1 / L)
    middle = math.log(2.0 / L)
    highest = math.log(0.05)
    slow_rates = jnp.exp(lowest + (middle - lowest) * jax.random.uniform(slow_key, (1, D), jnp.float32))
    fast_rates = jnp.exp(middle + (highest - middle) * jax.random.uniform(fast_key, (1, D), jnp.float32))
    portion = 0.5
    picked = jax.random.uniform(chooser, (1, D), jnp.float32) < portion
    rates = jnp.where(picked, slow_rates, fast_rates)
    position = jnp.arange(L, dtype=jnp.float32)[:, None]
    envelope = jnp.exp(-rates * position) * jnp.sqrt(-jnp.expm1(-2.0 * rates))
    noise = jnp.clip(jax.random.normal(noise_key, (L, D), jnp.float32), -4.0, 4.0)
    return jnp.clip(noise * envelope, -1.5, 1.5).astype(jnp.bfloat16)


def shard_levels(rng, shape, pieces, low, top_value):
    gain = 1.0
    for dim, blocks in pieces:
        draws = jax.random.uniform(jax.random.fold_in(jax.random.fold_in(rng, 6), dim), (blocks,), jnp.float32, low / len(pieces), top_value / len(pieces))
        gain = gain * jnp.repeat(jnp.exp(draws), shape[dim] // blocks).reshape((-1,) + (1,) * (len(shape) - 1 - dim))
    return gain


def bell_draw(key, dims, deviation, limit, cuts=(), kind=jnp.bfloat16):
    drawn = jax.random.normal(key, dims, jnp.float32) * deviation
    if len(cuts) > 0:
        drawn = shard_levels(key, dims, cuts, -0.22, 0.18) * drawn
    return jnp.clip(drawn, min=-limit, max=limit).astype(kind)


def setup_inputs(seed: int = 0) -> dict:
    seeds = jax.random.split(jax.random.key(seed), 7)
    query_in = bell_draw(seeds[0], (L, D), 1.0, 6.0, ((0, 16), (1, 2)))
    key_in = bell_draw(seeds[1], (L, D), 1.0, 6.0, ((0, 16), (1, 2)))
    value_in = bell_draw(seeds[2], (L, D), 1.0, 6.0, ((0, 16), (1, 2)))
    cotangent = draw_cotangent(jax.random.fold_in(seeds[6], 71), 0)
    short_weight = bell_draw(seeds[4], (3, KS, D), 0.5, 3.0, ((2, 2),), jnp.float32)
    long_filter = draw_long_filter(jax.random.fold_in(seeds[6], 71), 0)
    return {"query_in": query_in, "key_in": key_in, "value_in": value_in, "cotangent": cotangent, "short_weight": short_weight, "long_filter": long_filter}


def phase_grid(left_index, right_index, period):
    product = left_index[:, None] * right_index[None, :] % period
    phases = 2.0 * math.pi / period * product.astype(jnp.float32)
    return (jnp.cos(phases), jnp.sin(phases))

def short_filter(extended, weights, local_rows):
    tap_count = weights.shape[0]
    result = jnp.zeros((local_rows, extended.shape[1]), jnp.float32)
    for lag_index in range(tap_count):
        offset_row = tap_count - 1 - lag_index
        result = result + weights[lag_index] * extended[offset_row:offset_row + local_rows].astype(jnp.float32)
    return result

def filter_back(extended, weights, local_rows):
    tap_count = weights.shape[0]
    result = jnp.zeros((local_rows, extended.shape[1]), jnp.float32)
    for lag_index in range(tap_count):
        result = result + weights[lag_index] * extended[lag_index:lag_index + local_rows].astype(jnp.float32)
    return result

def weight_terms(grads, extended, tap_count, local_rows):
    grad_float = grads.astype(jnp.float32)
    terms = []
    for lag_index in range(tap_count):
        offset_row = tap_count - 1 - lag_index
        terms.append(lax.optimization_barrier(jnp.sum(grad_float * extended[offset_row:offset_row + local_rows].astype(jnp.float32), axis=0)))
    return jnp.stack(terms)

def reference(query_in, key_in, value_in, cotangent, short_weight, long_filter):
    length = L
    fft_size = 2 * L
    inner_len = S
    outer_len = fft_size // inner_len
    half_rows = outer_len // 2
    rim_rows = KS - 1
    outer_ids = jnp.arange(outer_len, dtype=jnp.int32)
    half_ids = jnp.arange(half_rows, dtype=jnp.int32)
    inner_ids = jnp.arange(inner_len, dtype=jnp.int32)
    cos_first, sin_first = phase_grid(outer_ids, half_ids, outer_len)
    cos_first = cos_first.astype(jnp.bfloat16).astype(jnp.float32)
    sin_first = sin_first.astype(jnp.bfloat16).astype(jnp.float32)
    cos_inner, sin_inner = phase_grid(inner_ids, inner_ids, inner_len)
    cos_inner = cos_inner.astype(jnp.bfloat16).astype(jnp.float32)
    sin_inner = sin_inner.astype(jnp.bfloat16).astype(jnp.float32)
    turn_cos, turn_sin = phase_grid(outer_ids, inner_ids, fft_size)
    turn_cos = turn_cos[:, :, None]
    turn_sin = turn_sin[:, :, None]
    chan_block = min(D, 256)
    block_count = D // chan_block
    inv_root = 1.0 / math.sqrt(length)

    def split_rows(values_in):
        return values_in.reshape(length, block_count, chan_block).transpose(1, 0, 2)

    def forward_transform(signal):
        grid_rows = signal.reshape(half_rows, inner_len, chan_block).astype(jnp.float32)
        first_re = jnp.einsum('kr,rsc->ksc', cos_first, grid_rows)
        first_im = -jnp.einsum('kr,rsc->ksc', sin_first, grid_rows)
        twist_re = (first_re * turn_cos + first_im * turn_sin).astype(jnp.bfloat16).astype(jnp.float32)
        twist_im = (first_im * turn_cos - first_re * turn_sin).astype(jnp.bfloat16).astype(jnp.float32)
        spec_re = jnp.einsum('js,ksc->kjc', cos_inner, twist_re) + jnp.einsum('js,ksc->kjc', sin_inner, twist_im)
        spec_im = jnp.einsum('js,ksc->kjc', cos_inner, twist_im) - jnp.einsum('js,ksc->kjc', sin_inner, twist_re)
        return (spec_re.astype(jnp.bfloat16), spec_im.astype(jnp.bfloat16))

    def inverse_transform(spec_re, spec_im):
        spec_re = spec_re.astype(jnp.float32)
        spec_im = spec_im.astype(jnp.float32)
        back_re = jnp.einsum('sj,kjc->ksc', cos_inner, spec_re) - jnp.einsum('sj,kjc->ksc', sin_inner, spec_im)
        back_im = jnp.einsum('sj,kjc->ksc', cos_inner, spec_im) + jnp.einsum('sj,kjc->ksc', sin_inner, spec_re)
        untw_re = (back_re * turn_cos - back_im * turn_sin).astype(jnp.bfloat16).astype(jnp.float32)
        untw_im = (back_im * turn_cos + back_re * turn_sin).astype(jnp.bfloat16).astype(jnp.float32)
        signal = jnp.einsum('kr,ksc->rsc', cos_first, untw_re) - jnp.einsum('kr,ksc->rsc', sin_first, untw_im)
        signal = (signal * (1.0 / fft_size)).astype(jnp.bfloat16)
        return signal.reshape(length, chan_block)

    def spectral_product(spec_re, spec_im, filt_re, filt_im):
        spec_re = spec_re.astype(jnp.float32)
        spec_im = spec_im.astype(jnp.float32)
        prod_re = spec_re * filt_re - spec_im * filt_im
        prod_im = spec_re * filt_im + spec_im * filt_re
        return (prod_re.astype(jnp.bfloat16), prod_im.astype(jnp.bfloat16))

    def one_block(inputs):
        query_blk, key_blk, value_blk, cot_blk, weights, filter_blk = inputs
        pad_rows = jnp.zeros((rim_rows, chan_block), jnp.bfloat16)
        ext_query = jnp.concatenate([pad_rows, query_blk], axis=0)
        ext_key = jnp.concatenate([pad_rows, key_blk], axis=0)
        ext_value = jnp.concatenate([pad_rows, value_blk], axis=0)
        q_short = short_filter(ext_query, weights[0], length)
        k_short = short_filter(ext_key, weights[1], length)
        v_short = short_filter(ext_value, weights[2], length)
        mixed = (k_short * v_short).astype(jnp.bfloat16)
        spec_h = forward_transform(filter_blk)
        h_re = spec_h[0].astype(jnp.float32)
        h_im = spec_h[1].astype(jnp.float32)
        spec_x = forward_transform(mixed)
        product = spectral_product(spec_x[0], spec_x[1], h_re, h_im)
        conv = inverse_transform(product[0], product[1]).astype(jnp.float32)
        block_out = (q_short * conv).astype(jnp.bfloat16)
        cot_float = cot_blk.astype(jnp.float32)
        gq_short = (cot_float * conv).astype(jnp.bfloat16)
        grad_conv = (cot_float * q_short).astype(jnp.bfloat16)
        spec_g = forward_transform(grad_conv)
        back_product = spectral_product(spec_g[0], spec_g[1], h_re, -h_im)
        grad_mixed = inverse_transform(back_product[0], back_product[1]).astype(jnp.float32)
        gk_short = (grad_mixed * v_short).astype(jnp.bfloat16)
        gv_short = (grad_mixed * k_short).astype(jnp.bfloat16)
        ext_gq = jnp.concatenate([gq_short, pad_rows], axis=0)
        ext_gk = jnp.concatenate([gk_short, pad_rows], axis=0)
        ext_gv = jnp.concatenate([gv_short, pad_rows], axis=0)
        grad_q = filter_back(ext_gq, weights[0], length).astype(jnp.bfloat16)
        grad_k = filter_back(ext_gk, weights[1], length).astype(jnp.bfloat16)
        grad_v = filter_back(ext_gv, weights[2], length).astype(jnp.bfloat16)
        short_part = jnp.stack([weight_terms(gq_short, ext_query, KS, length), weight_terms(gk_short, ext_key, KS, length), weight_terms(gv_short, ext_value, KS, length)])
        x_re = spec_x[0].astype(jnp.float32)
        x_im = spec_x[1].astype(jnp.float32)
        g_re = spec_g[0].astype(jnp.float32)
        g_im = spec_g[1].astype(jnp.float32)
        cross_re = ((g_re * x_re + g_im * x_im) * inv_root).astype(jnp.bfloat16)
        cross_im = ((g_im * x_re - g_re * x_im) * inv_root).astype(jnp.bfloat16)
        grad_filt = inverse_transform(cross_re, cross_im)
        grad_short_blk = short_part * inv_root
        return (block_out, grad_q, grad_k, grad_v, grad_short_blk, grad_filt)
    weight_blocks = short_weight.reshape(3, KS, block_count, chan_block).transpose(2, 0, 1, 3)
    results = lax.map(one_block, (split_rows(query_in), split_rows(key_in), split_rows(value_in), split_rows(cotangent), weight_blocks, split_rows(long_filter)))

    def join_rows(values_in):
        return values_in.transpose(1, 0, 2).reshape(length, D)
    grad_short = results[4].transpose(1, 2, 0, 3).reshape(3, KS, D)
    return (join_rows(results[0]), join_rows(results[1]), join_rows(results[2]), join_rows(results[3]), grad_short, join_rows(results[5]))
```

```python
import functools
import math

import jax
import jax.numpy as jnp
import numpy as np
from jax import lax
from jax.experimental import pallas as pl
from jax.experimental.pallas import tpu as pltpu
from jax.sharding import PartitionSpec as P

S = 128
G = 16
LANES = 128


def from_behind(x, axis, by):
    count = lax.axis_size(axis)
    pairs = [(i, i + by) for i in range(count) if 0 <= i + by < count]
    return lax.ppermute(x, axis, pairs)


def short_filter(extended, weights, local_rows):
    tap_count = weights.shape[0]
    result = jnp.zeros((local_rows, extended.shape[1]), jnp.float32)
    for lag_index in range(tap_count):
        offset_row = tap_count - 1 - lag_index
        result = result + weights[lag_index] * extended[
            offset_row : offset_row + local_rows
        ].astype(jnp.float32)
    return result


def filter_back(extended, weights, local_rows):
    tap_count = weights.shape[0]
    result = jnp.zeros((local_rows, extended.shape[1]), jnp.float32)
    for lag_index in range(tap_count):
        result = result + weights[lag_index] * extended[lag_index : lag_index + local_rows].astype(
            jnp.float32
        )
    return result


def weight_terms(grads, extended, tap_count, local_rows):
    grad_float = grads.astype(jnp.float32)
    terms = []
    for lag_index in range(tap_count):
        offset_row = tap_count - 1 - lag_index
        terms.append(
            jnp.sum(
                grad_float * extended[offset_row : offset_row + local_rows].astype(jnp.float32),
                axis=0,
            )
        )
    return jnp.stack(terms)


def grid_tables(outer_len):
    half_rows = outer_len // 2
    k_count = half_rows + 1
    k_ids = np.arange(k_count)[:, None]
    r_ids = np.arange(half_rows)[None, :]
    angle = 2.0 * np.pi / outer_len * (k_ids * r_ids % outer_len)
    first = np.concatenate([np.cos(angle), -np.sin(angle)[1:half_rows]], axis=0)
    weight = np.full((k_count, 1), 2.0)
    weight[0] = weight[half_rows] = 1.0
    back = np.concatenate([weight * np.cos(angle), -2.0 * np.sin(angle)[1:half_rows]], axis=0).T
    inner = 2.0 * np.pi / S * (np.arange(S)[:, None] * np.arange(S)[None, :] % S)
    cos, sin = np.cos(inner), np.sin(inner)
    inner_fwd = np.block([[cos, sin], [-sin, cos]])
    inner_back = np.block([[cos, -sin], [sin, cos]])
    turn = 2.0 * np.pi / (outer_len * S) * (k_ids * np.arange(S)[None, :])
    return first, back, inner_fwd, inner_back, np.cos(turn), np.sin(turn)


def spread_over_rows(table):
    return jnp.asarray(np.kron(table, np.eye(G)).astype(jnp.bfloat16))


def spectral_kernel(
    inv_root,
    scale,
    xg_ref,
    h_ref,
    first_ref,
    back_ref,
    inner_fwd_ref,
    inner_back_ref,
    cos_ref,
    sin_ref,
    cg_ref,
    gf_ref,
    work,
):
    k_count = work.shape[0]
    half_rows = k_count - 1
    rows_per = h_ref.shape[1] // S

    def first_section(step, carry):
        at = pl.multiple_of(step * G, G)
        pieces = []
        for r in range(half_rows):
            rows = pl.ds((r % rows_per) * S + at, G)
            pieces.append(
                jnp.concatenate(
                    [
                        xg_ref[r // rows_per, 0, rows, :],
                        xg_ref[r // rows_per, 1, rows, :],
                        h_ref[r // rows_per, rows, :],
                    ],
                    axis=1,
                )
            )
        grid_rows = jnp.concatenate(pieces, axis=0)
        first = jnp.dot(first_ref[...], grid_rows, preferred_element_type=jnp.float32)
        for k in range(k_count):
            re = first[k * G : (k + 1) * G]
            cos = jnp.concatenate([cos_ref[k, pl.ds(at, G), :]] * 3, axis=1)
            sin = jnp.concatenate([sin_ref[k, pl.ds(at, G), :]] * 3, axis=1)
            if 0 < k < half_rows:
                row = (k_count + k - 1) * G
                im = first[row : row + G]
                turned_re = re * cos + im * sin
                turned_im = im * cos - re * sin
            else:
                turned_re = re * cos
                turned_im = -re * sin
            work[k, pl.ds(at, G), :] = turned_re.astype(jnp.bfloat16)
            work[k, pl.ds(S + at, G), :] = turned_im.astype(jnp.bfloat16)
        return carry

    lax.fori_loop(0, S // G, first_section, 0)

    def one_row(k):
        spec = jnp.dot(inner_fwd_ref[...], work[k], preferred_element_type=jnp.float32)
        spec = spec.astype(jnp.bfloat16).astype(jnp.float32)
        x_re, x_im = spec[:S, :LANES], spec[S:, :LANES]
        g_re, g_im = spec[:S, LANES : 2 * LANES], spec[S:, LANES : 2 * LANES]
        h_re, h_im = spec[:S, 2 * LANES :], spec[S:, 2 * LANES :]
        real = jnp.concatenate(
            [
                x_re * h_re - x_im * h_im,
                g_re * h_re + g_im * h_im,
                (g_re * x_re + g_im * x_im) * inv_root,
            ],
            axis=1,
        )
        imag = jnp.concatenate(
            [
                x_re * h_im + x_im * h_re,
                g_im * h_re - g_re * h_im,
                (g_im * x_re - g_re * x_im) * inv_root,
            ],
            axis=1,
        )
        product = jnp.concatenate([real, imag], axis=0).astype(jnp.bfloat16)
        back = jnp.dot(inner_back_ref[...], product, preferred_element_type=jnp.float32)
        cos = jnp.concatenate([cos_ref[k]] * 3, axis=1)
        sin = jnp.concatenate([sin_ref[k]] * 3, axis=1)
        work[k, :S, :] = (back[:S] * cos - back[S:] * sin).astype(jnp.bfloat16)
        work[k, S:, :] = (back[S:] * cos + back[:S] * sin).astype(jnp.bfloat16)

    batch = next(n for n in (3, 5, 1) if k_count % n == 0)

    def some_rows(step, carry):
        for i in range(batch):
            one_row(step * batch + i)
        return carry

    lax.fori_loop(0, k_count // batch, some_rows, 0)

    def last_section(step, carry):
        at = pl.multiple_of(step * G, G)
        pieces = [work[k, pl.ds(at, G), :] for k in range(k_count)]
        pieces += [work[k, pl.ds(S + at, G), :] for k in range(1, half_rows)]
        signal = jnp.dot(
            back_ref[...], jnp.concatenate(pieces, axis=0), preferred_element_type=jnp.float32
        )
        signal = (signal * scale).astype(jnp.bfloat16)
        for r in range(half_rows):
            rows = pl.ds((r % rows_per) * S + at, G)
            part = signal[r * G : (r + 1) * G]
            cg_ref[r // rows_per, 0, rows, :] = part[:, :LANES]
            cg_ref[r // rows_per, 1, rows, :] = part[:, LANES : 2 * LANES]
            gf_ref[r // rows_per, rows, :] = part[:, 2 * LANES :]
        return carry

    lax.fori_loop(0, S // G, last_section, 0)


def transform_chunk(xg, h, tables, inv_root, scale):
    k_count = tables[4].shape[0]
    lanes = h.shape[-1]
    if lanes < LANES:
        xg = jnp.pad(xg, ((0, 0),) * 3 + ((0, LANES - lanes),))
        h = jnp.pad(h, ((0, 0),) * 2 + ((0, LANES - lanes),))
    cg, gf = pl.pallas_call(
        functools.partial(spectral_kernel, inv_root, scale),
        out_shape=(
            jax.ShapeDtypeStruct(xg.shape, jnp.bfloat16),
            jax.ShapeDtypeStruct(h.shape, jnp.bfloat16),
        ),
        in_specs=[pl.BlockSpec(memory_space=pltpu.VMEM)] * 8,
        out_specs=(pl.BlockSpec(memory_space=pltpu.VMEM),) * 2,
        scratch_shapes=[pltpu.VMEM((k_count, 2 * S, 3 * LANES), jnp.bfloat16)],
        compiler_params=pltpu.CompilerParams(vmem_limit_bytes=58 * 1024 * 1024),
        cost_estimate=pl.CostEstimate(
            flops=13_000_000_000, bytes_accessed=16_000_000, transcendentals=0
        ),
    )(xg, h, *tables)
    return cg[..., :lanes], gf[..., :lanes]


def exchange(x):
    return lax.all_to_all(x, "ctx", split_axis=0, concat_axis=0, tiled=True)


def sum_over(x, axis):
    count = lax.axis_size(axis)
    step = 1
    while step < count:
        x = x + lax.ppermute(x, axis, [(i, i ^ step) for i in range(count)])
        step *= 2
    return x


def on_device(query_in, key_in, value_in, cotangent, short_weight, long_filter):
    local_rows, channels = query_in.shape
    tap_count = short_weight.shape[1]
    rim_rows = tap_count - 1
    ctx_size = lax.axis_size("ctx")
    length = local_rows * ctx_size
    fft_size = 2 * length
    outer_len = fft_size // S
    inv_root = 1.0 / math.sqrt(length)
    own = channels // ctx_size
    lanes = min(own, LANES)
    chunks = own // lanes

    def to_owners(x):
        return x.reshape(local_rows, ctx_size, chunks, lanes).transpose(2, 1, 0, 3)

    def from_owners(parts):
        return jnp.stack(parts).transpose(2, 1, 0, 3).reshape(local_rows, channels)

    first, back, inner_fwd, inner_back, turn_cos, turn_sin = grid_tables(outer_len)
    tables = (
        spread_over_rows(first),
        spread_over_rows(back),
        jnp.asarray(inner_fwd, jnp.bfloat16),
        jnp.asarray(inner_back, jnp.bfloat16),
        jnp.broadcast_to(
            jnp.asarray(turn_cos, jnp.float32)[:, :, None], turn_cos.shape + (LANES,)
        ),
        jnp.broadcast_to(
            jnp.asarray(turn_sin, jnp.float32)[:, :, None], turn_sin.shape + (LANES,)
        ),
    )
    filter_parts = to_owners(long_filter)
    h_parts = [exchange(filter_parts[c]) for c in range(chunks)]
    ahead = from_behind(
        (
            query_in[local_rows - rim_rows :],
            key_in[local_rows - rim_rows :],
            value_in[local_rows - rim_rows :],
        ),
        "ctx",
        1,
    )
    ext_query = jnp.concatenate([ahead[0], query_in], axis=0)
    ext_key = jnp.concatenate([ahead[1], key_in], axis=0)
    ext_value = jnp.concatenate([ahead[2], value_in], axis=0)
    q_short = short_filter(ext_query, short_weight[0], local_rows)
    k_short = short_filter(ext_key, short_weight[1], local_rows)
    v_short = short_filter(ext_value, short_weight[2], local_rows)
    mixed = (k_short * v_short).astype(jnp.bfloat16)
    cot_float = cotangent.astype(jnp.float32)
    grad_conv = (cot_float * q_short).astype(jnp.bfloat16)
    xg_parts = jnp.stack([to_owners(mixed), to_owners(grad_conv)], axis=2)
    xg_parts = [exchange(xg_parts[c]) for c in range(chunks)]
    cg_parts, gf_parts = [], []
    for xg, h in zip(xg_parts, h_parts):
        cg, gf = transform_chunk(xg, h, tables, inv_root, 1.0 / fft_size)
        cg_parts.append(exchange(cg))
        gf_parts.append(gf)
    gf_parts = [exchange(gf) for gf in gf_parts]
    conv = from_owners([part[:, 0] for part in cg_parts]).astype(jnp.float32)
    grad_mixed = from_owners([part[:, 1] for part in cg_parts]).astype(jnp.float32)
    grad_filter = from_owners(gf_parts)
    block_out = (q_short * conv).astype(jnp.bfloat16)
    gq_short = (cot_float * conv).astype(jnp.bfloat16)
    gk_short = (grad_mixed * v_short).astype(jnp.bfloat16)
    gv_short = (grad_mixed * k_short).astype(jnp.bfloat16)
    behind = from_behind((gq_short[:rim_rows], gk_short[:rim_rows], gv_short[:rim_rows]), "ctx", -1)
    ext_gq = jnp.concatenate([gq_short, behind[0]], axis=0)
    ext_gk = jnp.concatenate([gk_short, behind[1]], axis=0)
    ext_gv = jnp.concatenate([gv_short, behind[2]], axis=0)
    grad_query = filter_back(ext_gq, short_weight[0], local_rows).astype(jnp.bfloat16)
    grad_key = filter_back(ext_gk, short_weight[1], local_rows).astype(jnp.bfloat16)
    grad_value = filter_back(ext_gv, short_weight[2], local_rows).astype(jnp.bfloat16)
    short_part = jnp.stack(
        [
            weight_terms(gq_short, ext_query, tap_count, local_rows),
            weight_terms(gk_short, ext_key, tap_count, local_rows),
            weight_terms(gv_short, ext_value, tap_count, local_rows),
        ]
    )
    grad_short = sum_over(short_part, "ctx") * inv_root
    return (block_out, grad_query, grad_key, grad_value, grad_short, grad_filter)


def solution(mesh):
    in_specs = (
        P("ctx", "tp"),
        P("ctx", "tp"),
        P("ctx", "tp"),
        P("ctx", "tp"),
        P(None, None, "tp"),
        P("ctx", "tp"),
    )
    out_specs = (
        P("ctx", "tp"),
        P("ctx", "tp"),
        P("ctx", "tp"),
        P("ctx", "tp"),
        P(None, None, "tp"),
        P("ctx", "tp"),
    )
    return jax.shard_map(
        on_device, mesh=mesh, in_specs=in_specs, out_specs=out_specs, check_vma=False
    )
```

```python
import functools
import math

import jax
import jax.numpy as jnp
import numpy as np
from jax import lax
from jax.experimental import pallas as pl
from jax.experimental.pallas import tpu as pltpu
from jax.sharding import PartitionSpec as P

S = 128
G = 16
LANES = 128


def from_behind(x, axis, by):
    count = lax.axis_size(axis)
    pairs = [(i, i + by) for i in range(count) if 0 <= i + by < count]
    return lax.ppermute(x, axis, pairs)


def grid_tables(outer_len):
    half_rows = outer_len // 2
    k_count = half_rows + 1
    k_ids = np.arange(k_count)[:, None]
    r_ids = np.arange(half_rows)[None, :]
    angle = 2.0 * np.pi / outer_len * (k_ids * r_ids % outer_len)
    first = np.concatenate([np.cos(angle), -np.sin(angle)[1:half_rows]], axis=0)
    weight = np.full((k_count, 1), 2.0)
    weight[0] = weight[half_rows] = 1.0
    back = np.concatenate([weight * np.cos(angle), -2.0 * np.sin(angle)[1:half_rows]], axis=0).T
    inner = 2.0 * np.pi / S * (np.arange(S)[:, None] * np.arange(S)[None, :] % S)
    cos, sin = np.cos(inner), np.sin(inner)
    inner_fwd = np.block([[cos, sin], [-sin, cos]])
    inner_back = np.block([[cos, -sin], [sin, cos]])
    turn = 2.0 * np.pi / (outer_len * S) * (k_ids * np.arange(S)[None, :])
    return first, back, inner_fwd, inner_back, np.cos(turn), np.sin(turn)


def spread_over_rows(table):
    return jnp.asarray(np.kron(table, np.eye(G)).astype(jnp.bfloat16))


def spectral_kernel(
    inv_root,
    scale,
    chunk,
    xg_ref,
    h_ref,
    first_ref,
    back_ref,
    inner_fwd_ref,
    inner_back_ref,
    cos_ref,
    sin_ref,
    cg_ref,
    gf_ref,
    work,
):
    k_count = work.shape[0]
    half_rows = k_count - 1
    rows_per = h_ref.shape[2] // S

    def first_section(step, carry):
        at = pl.multiple_of(step * G, G)
        pieces = []
        for r in range(half_rows):
            rows = pl.ds((r % rows_per) * S + at, G)
            pieces.append(
                jnp.concatenate(
                    [
                        xg_ref[r // rows_per, 0, rows, :],
                        xg_ref[r // rows_per, 1, rows, :],
                        h_ref[r // rows_per, chunk, rows, :],
                    ],
                    axis=1,
                )
            )
        grid_rows = jnp.concatenate(pieces, axis=0)
        first = jnp.dot(first_ref[...], grid_rows, preferred_element_type=jnp.float32)
        for k in range(k_count):
            re = first[k * G : (k + 1) * G]
            cos = jnp.concatenate([cos_ref[k, pl.ds(at, G), :]] * 3, axis=1)
            sin = jnp.concatenate([sin_ref[k, pl.ds(at, G), :]] * 3, axis=1)
            if 0 < k < half_rows:
                row = (k_count + k - 1) * G
                im = first[row : row + G]
                turned_re = re * cos + im * sin
                turned_im = im * cos - re * sin
            else:
                turned_re = re * cos
                turned_im = -re * sin
            work[k, pl.ds(at, G), :] = turned_re.astype(jnp.bfloat16)
            work[k, pl.ds(S + at, G), :] = turned_im.astype(jnp.bfloat16)
        return carry

    lax.fori_loop(0, S // G, first_section, 0)

    def one_row(k):
        spec = jnp.dot(inner_fwd_ref[...], work[k], preferred_element_type=jnp.float32)
        spec = spec.astype(jnp.bfloat16).astype(jnp.float32)
        x_re, x_im = spec[:S, :LANES], spec[S:, :LANES]
        g_re, g_im = spec[:S, LANES : 2 * LANES], spec[S:, LANES : 2 * LANES]
        h_re, h_im = spec[:S, 2 * LANES :], spec[S:, 2 * LANES :]
        real = jnp.concatenate(
            [
                x_re * h_re - x_im * h_im,
                g_re * h_re + g_im * h_im,
                (g_re * x_re + g_im * x_im) * inv_root,
            ],
            axis=1,
        )
        imag = jnp.concatenate(
            [
                x_re * h_im + x_im * h_re,
                g_im * h_re - g_re * h_im,
                (g_im * x_re - g_re * x_im) * inv_root,
            ],
            axis=1,
        )
        product = jnp.concatenate([real, imag], axis=0).astype(jnp.bfloat16)
        back = jnp.dot(inner_back_ref[...], product, preferred_element_type=jnp.float32)
        cos = jnp.concatenate([cos_ref[k]] * 3, axis=1)
        sin = jnp.concatenate([sin_ref[k]] * 3, axis=1)
        work[k, :S, :] = (back[:S] * cos - back[S:] * sin).astype(jnp.bfloat16)
        work[k, S:, :] = (back[S:] * cos + back[:S] * sin).astype(jnp.bfloat16)

    batch = next(n for n in (3, 5, 1) if k_count % n == 0)

    def some_rows(step, carry):
        for i in range(batch):
            one_row(step * batch + i)
        return carry

    lax.fori_loop(0, k_count // batch, some_rows, 0)

    def last_section(step, carry):
        at = pl.multiple_of(step * G, G)
        pieces = [work[k, pl.ds(at, G), :] for k in range(k_count)]
        pieces += [work[k, pl.ds(S + at, G), :] for k in range(1, half_rows)]
        signal = jnp.dot(
            back_ref[...], jnp.concatenate(pieces, axis=0), preferred_element_type=jnp.float32
        )
        signal = (signal * scale).astype(jnp.bfloat16)
        for r in range(half_rows):
            rows = pl.ds((r % rows_per) * S + at, G)
            part = signal[r * G : (r + 1) * G]
            cg_ref[r // rows_per, 0, rows, :] = part[:, :LANES]
            cg_ref[r // rows_per, 1, rows, :] = part[:, LANES : 2 * LANES]
            gf_ref[r // rows_per, rows, :] = part[:, 2 * LANES :]
        return carry

    lax.fori_loop(0, S // G, last_section, 0)


def transform_chunk(xg, h, chunk, tables, inv_root, scale):
    k_count = tables[4].shape[0]
    lanes = h.shape[-1]
    if lanes < LANES:
        xg = jnp.pad(xg, ((0, 0),) * 3 + ((0, LANES - lanes),))
        h = jnp.pad(h, ((0, 0),) * 3 + ((0, LANES - lanes),))
    cg, gf = pl.pallas_call(
        functools.partial(spectral_kernel, inv_root, scale, chunk),
        out_shape=(
            jax.ShapeDtypeStruct(xg.shape, jnp.bfloat16),
            jax.ShapeDtypeStruct((h.shape[0],) + h.shape[2:], jnp.bfloat16),
        ),
        in_specs=[pl.BlockSpec(memory_space=pltpu.VMEM)] * 8,
        out_specs=(pl.BlockSpec(memory_space=pltpu.VMEM),) * 2,
        scratch_shapes=[pltpu.VMEM((k_count, 2 * S, 3 * LANES), jnp.bfloat16)],
        compiler_params=pltpu.CompilerParams(vmem_limit_bytes=58 * 1024 * 1024),
        cost_estimate=pl.CostEstimate(
            flops=13_000_000_000, bytes_accessed=16_000_000, transcendentals=0
        ),
    )(xg, h, *tables)
    return cg[..., :lanes], gf[..., :lanes]


def later(x, head):
    row = lax.broadcasted_iota(jnp.int32, x.shape, 0)
    one = jnp.where(row == 0, head[1:2], pltpu.roll(x, 1, 0))
    two = jnp.where(row == 0, head[0:1], jnp.where(row == 1, head[1:2], pltpu.roll(x, 2, 0)))
    return (x, one, two)


def sooner(x, tail):
    count = x.shape[0]
    row = lax.broadcasted_iota(jnp.int32, x.shape, 0)
    one = jnp.where(row == count - 1, tail[0:1], pltpu.roll(x, count - 1, 0))
    two = jnp.where(
        row == count - 1,
        tail[1:2],
        jnp.where(row == count - 2, tail[0:1], pltpu.roll(x, count - 2, 0)),
    )
    return (x, one, two)


def weigh(shifted, weights):
    return sum(weights[j : j + 1] * shifted[j] for j in range(len(shifted)))


def as_float(ref):
    return ref[...].astype(jnp.float32)


def rounded(x):
    return x.astype(jnp.bfloat16)


def filter_kernel(h_ref, out_ref):
    per, chunks, _, lanes = out_ref.shape
    for i in range(per):
        for c in range(chunks):
            at = (i * chunks + c) * lanes
            out_ref[i, c] = h_ref[:, at : at + lanes]


def unpack_kernel(gf_ref, out_ref):
    per, chunks, _, lanes = gf_ref.shape
    for i in range(per):
        for c in range(chunks):
            at = (i * chunks + c) * lanes
            out_ref[:, at : at + lanes] = gf_ref[i, c]


def entry_kernel(q_ref, k_ref, v_ref, cot_ref, ahead_ref, w_ref, *outs):
    ahead = as_float(ahead_ref)
    per, _, _, lanes = outs[0].shape
    shorts = []
    for i, ref in enumerate((q_ref, k_ref, v_ref)):
        shorts.append(weigh(later(as_float(ref), ahead[2 * i : 2 * i + 2]), w_ref[i]))
    mixed = rounded(shorts[1] * shorts[2])
    grad_conv = rounded(as_float(cot_ref) * shorts[0])
    for i in range(per):
        for c, out in enumerate(outs):
            at = (i * len(outs) + c) * lanes
            out[i, 0] = mixed[:, at : at + lanes]
            out[i, 1] = grad_conv[:, at : at + lanes]


def local_grads(q_ref, k_ref, v_ref, cot_ref, ahead_ref, w_ref, conv, grad_mixed):
    ahead = as_float(ahead_ref)
    shifted = []
    shorts = []
    for i, ref in enumerate((q_ref, k_ref, v_ref)):
        shifted.append(later(as_float(ref), ahead[2 * i : 2 * i + 2]))
        shorts.append(weigh(shifted[i], w_ref[i]))
    grads = [as_float(cot_ref) * conv, grad_mixed * shorts[2], grad_mixed * shorts[1]]
    grads = [rounded(g).astype(jnp.float32) for g in grads]
    return shifted, shorts, grads


def gather_lanes(cg_refs, which, blocks):
    parts = [cg[i, which] for i in blocks for cg in cg_refs]
    return jnp.concatenate(parts, axis=1).astype(jnp.float32)


def edge_kernel(q_ref, k_ref, v_ref, cot_ref, ahead_ref, w_ref, *rest):
    cg_refs, edge_ref = rest[:-1], rest[-1]
    blocks = range(cg_refs[0].shape[0])
    conv = gather_lanes(cg_refs, 0, blocks)
    grad_mixed = gather_lanes(cg_refs, 1, blocks)
    _, _, grads = local_grads(
        q_ref, k_ref, v_ref, cot_ref, ahead_ref, w_ref, conv, grad_mixed
    )
    for i in range(3):
        edge_ref[2 * i : 2 * i + 2, :] = rounded(grads[i][:2])


def exit_kernel(chunks, q_ref, k_ref, v_ref, cot_ref, ahead_ref, w_ref, behind_ref, *rest):
    cg_refs = rest[:chunks]
    out_ref, gq_ref, gk_ref, gv_ref, short_ref = rest[chunks:]
    blocks = range(cg_refs[0].shape[0])
    conv = gather_lanes(cg_refs, 0, blocks)
    grad_mixed = gather_lanes(cg_refs, 1, blocks)
    shifted, shorts, grads = local_grads(
        q_ref, k_ref, v_ref, cot_ref, ahead_ref, w_ref, conv, grad_mixed
    )
    out_ref[...] = rounded(shorts[0] * conv)
    behind = as_float(behind_ref)
    for i, ref in enumerate((gq_ref, gk_ref, gv_ref)):
        ref[...] = rounded(weigh(sooner(grads[i], behind[2 * i : 2 * i + 2]), w_ref[i]))
        for j in range(3):
            short_ref[i, j : j + 1, :] = jnp.sum(grads[i] * shifted[i][j], axis=0, keepdims=True)


def exchange(x):
    return lax.all_to_all(x, "ctx", split_axis=0, concat_axis=0, tiled=True)


def sum_over(x, axis):
    count = lax.axis_size(axis)
    step = 1
    while step < count:
        x = x + lax.ppermute(x, axis, [(i, i ^ step) for i in range(count)])
        step *= 2
    return x


def on_device(query_in, key_in, value_in, cotangent, short_weight, long_filter):
    local_rows, channels = query_in.shape
    tap_count = short_weight.shape[1]
    rim_rows = tap_count - 1
    ctx_size = lax.axis_size("ctx")
    length = local_rows * ctx_size
    fft_size = 2 * length
    outer_len = fft_size // S
    inv_root = 1.0 / math.sqrt(length)
    own = channels // ctx_size
    lanes = min(own, LANES)
    chunks = own // lanes
    width = max(own, LANES)
    per = width // own
    steps = channels // width
    limit = pltpu.CompilerParams(vmem_limit_bytes=58 * 1024 * 1024)
    stream = pl.BlockSpec((local_rows, width), lambda i: (0, i))
    rim = pl.BlockSpec((3 * rim_rows, width), lambda i: (0, i))
    taps = pl.BlockSpec((3, tap_count, width), lambda i: (0, 0, i))
    pair = pl.BlockSpec((per, 2, local_rows, lanes), lambda i: (i, 0, 0, 0))
    packed = pl.BlockSpec((per, chunks, local_rows, lanes), lambda i: (i, 0, 0, 0))
    whole = jax.ShapeDtypeStruct((local_rows, channels), jnp.bfloat16)

    first, back, inner_fwd, inner_back, turn_cos, turn_sin = grid_tables(outer_len)
    tables = (
        spread_over_rows(first),
        spread_over_rows(back),
        jnp.asarray(inner_fwd, jnp.bfloat16),
        jnp.asarray(inner_back, jnp.bfloat16),
        jnp.broadcast_to(
            jnp.asarray(turn_cos, jnp.float32)[:, :, None], turn_cos.shape + (LANES,)
        ),
        jnp.broadcast_to(
            jnp.asarray(turn_sin, jnp.float32)[:, :, None], turn_sin.shape + (LANES,)
        ),
    )
    tails = jnp.concatenate([x[local_rows - rim_rows :] for x in (query_in, key_in, value_in)])
    ahead = from_behind(tails, "ctx", 1)
    h = exchange(
        pl.pallas_call(
            filter_kernel,
            grid=(steps,),
            out_shape=jax.ShapeDtypeStruct((ctx_size, chunks, local_rows, lanes), jnp.bfloat16),
            in_specs=[stream],
            out_specs=packed,
            compiler_params=limit,
        )(long_filter)
    )
    streams = (query_in, key_in, value_in, cotangent, ahead, short_weight)
    xg_parts = pl.pallas_call(
        entry_kernel,
        grid=(steps,),
        out_shape=(
            jax.ShapeDtypeStruct((ctx_size, 2, local_rows, lanes), jnp.bfloat16),
        )
        * chunks,
        in_specs=[stream] * 4 + [rim, taps],
        out_specs=(pair,) * chunks,
        compiler_params=limit,
        cost_estimate=pl.CostEstimate(
            flops=100_000_000, bytes_accessed=12_000_000, transcendentals=0
        ),
    )(*streams)
    xg_parts = [exchange(xg) for xg in xg_parts]
    cg_parts, gf_parts = [], []
    for c, xg in enumerate(xg_parts):
        cg, gf = transform_chunk(xg, h, c, tables, inv_root, 1.0 / fft_size)
        cg_parts.append(exchange(cg))
        gf_parts.append(gf)
    gf_back = exchange(jnp.stack(gf_parts, axis=1))
    top = pl.BlockSpec((G, channels), lambda i: (0, 0))
    edge = pl.pallas_call(
        edge_kernel,
        grid=(1,),
        out_shape=jax.ShapeDtypeStruct((3 * rim_rows, channels), jnp.bfloat16),
        in_specs=[top] * 4
        + [
            pl.BlockSpec((3 * rim_rows, channels), lambda i: (0, 0)),
            pl.BlockSpec((3, tap_count, channels), lambda i: (0, 0, 0)),
        ]
        + [pl.BlockSpec((ctx_size, 2, G, lanes), lambda i: (0, 0, 0, 0))] * chunks,
        out_specs=pl.BlockSpec((3 * rim_rows, channels), lambda i: (0, 0)),
        compiler_params=limit,
    )(*streams, *cg_parts)
    behind = from_behind(edge, "ctx", -1)
    block_out, grad_query, grad_key, grad_value, short_part = pl.pallas_call(
        functools.partial(exit_kernel, chunks),
        grid=(steps,),
        out_shape=(whole,) * 4 + (jax.ShapeDtypeStruct((3, tap_count, channels), jnp.float32),),
        in_specs=[stream] * 4 + [rim, taps, rim] + [pair] * chunks,
        out_specs=(stream,) * 4 + (taps,),
        compiler_params=limit,
        cost_estimate=pl.CostEstimate(
            flops=200_000_000, bytes_accessed=20_000_000, transcendentals=0
        ),
    )(*streams, behind, *cg_parts)
    grad_short = sum_over(short_part, "ctx") * inv_root
    grad_filter = pl.pallas_call(
        unpack_kernel,
        grid=(steps,),
        out_shape=whole,
        in_specs=[packed],
        out_specs=stream,
        compiler_params=limit,
    )(gf_back)
    return (block_out, grad_query, grad_key, grad_value, grad_short, grad_filter)


def solution(mesh):
    in_specs = (
        P("ctx", "tp"),
        P("ctx", "tp"),
        P("ctx", "tp"),
        P("ctx", "tp"),
        P(None, None, "tp"),
        P("ctx", "tp"),
    )
    out_specs = (
        P("ctx", "tp"),
        P("ctx", "tp"),
        P("ctx", "tp"),
        P("ctx", "tp"),
        P(None, None, "tp"),
        P("ctx", "tp"),
    )
    return jax.shard_map(
        on_device, mesh=mesh, in_specs=in_specs, out_specs=out_specs, check_vma=False
    )
```

```python
import functools
import math

import jax
import jax.numpy as jnp
import numpy as np
from jax import lax
from jax.experimental import pallas as pl
from jax.experimental.pallas import tpu as pltpu
from jax.sharding import PartitionSpec as P

S = 128
G = 16
LANES = 128


def from_behind(x, axis, by):
    count = lax.axis_size(axis)
    pairs = [(i, i + by) for i in range(count) if 0 <= i + by < count]
    return lax.ppermute(x, axis, pairs)


def grid_tables(outer_len):
    half_rows = outer_len // 2
    k_count = half_rows + 1
    k_ids = np.arange(k_count)[:, None]
    r_ids = np.arange(half_rows)[None, :]
    angle = 2.0 * np.pi / outer_len * (k_ids * r_ids % outer_len)
    first = np.concatenate([np.cos(angle), -np.sin(angle)[1:half_rows]], axis=0)
    weight = np.full((k_count, 1), 2.0)
    weight[0] = weight[half_rows] = 1.0
    back = np.concatenate([weight * np.cos(angle), -2.0 * np.sin(angle)[1:half_rows]], axis=0).T
    inner = 2.0 * np.pi / S * (np.arange(S)[:, None] * np.arange(S)[None, :] % S)
    cos, sin = np.cos(inner), np.sin(inner)
    inner_fwd = np.block([[cos, sin], [-sin, cos]])
    inner_back = np.block([[cos, -sin], [sin, cos]])
    turn = 2.0 * np.pi / (outer_len * S) * (k_ids * np.arange(S)[None, :])
    return first, back, inner_fwd, inner_back, np.cos(turn), np.sin(turn)


def spread_over_rows(table):
    return jnp.asarray(np.kron(table, np.eye(G)).astype(jnp.bfloat16))


def spectral_kernel(
    inv_root,
    scale,
    xg_ref,
    first_ref,
    back_ref,
    inner_fwd_ref,
    inner_back_ref,
    cos_ref,
    sin_ref,
    cg_ref,
    gf_ref,
    work,
):
    k_count = work.shape[0]
    half_rows = k_count - 1
    rows_per = xg_ref.shape[2] // S

    def first_section(step, carry):
        at = pl.multiple_of(step * G, G)
        pieces = []
        for r in range(half_rows):
            rows = pl.ds((r % rows_per) * S + at, G)
            pieces.append(
                jnp.concatenate(
                    [
                        xg_ref[r // rows_per, 0, rows, :],
                        xg_ref[r // rows_per, 1, rows, :],
                        xg_ref[r // rows_per, 2, rows, :],
                    ],
                    axis=1,
                )
            )
        grid_rows = jnp.concatenate(pieces, axis=0)
        first = jnp.dot(first_ref[...], grid_rows, preferred_element_type=jnp.float32)
        for k in range(k_count):
            re = first[k * G : (k + 1) * G]
            cos = jnp.concatenate([cos_ref[k, pl.ds(at, G), :]] * 3, axis=1)
            sin = jnp.concatenate([sin_ref[k, pl.ds(at, G), :]] * 3, axis=1)
            if 0 < k < half_rows:
                row = (k_count + k - 1) * G
                im = first[row : row + G]
                turned_re = re * cos + im * sin
                turned_im = im * cos - re * sin
            else:
                turned_re = re * cos
                turned_im = -re * sin
            work[k, pl.ds(at, G), :] = turned_re.astype(jnp.bfloat16)
            work[k, pl.ds(S + at, G), :] = turned_im.astype(jnp.bfloat16)
        return carry

    lax.fori_loop(0, S // G, first_section, 0)

    def one_row(k):
        spec = jnp.dot(inner_fwd_ref[...], work[k], preferred_element_type=jnp.float32)
        spec = spec.astype(jnp.bfloat16).astype(jnp.float32)
        x_re, x_im = spec[:S, :LANES], spec[S:, :LANES]
        g_re, g_im = spec[:S, LANES : 2 * LANES], spec[S:, LANES : 2 * LANES]
        h_re, h_im = spec[:S, 2 * LANES :], spec[S:, 2 * LANES :]
        real = jnp.concatenate(
            [
                x_re * h_re - x_im * h_im,
                g_re * h_re + g_im * h_im,
                (g_re * x_re + g_im * x_im) * inv_root,
            ],
            axis=1,
        )
        imag = jnp.concatenate(
            [
                x_re * h_im + x_im * h_re,
                g_im * h_re - g_re * h_im,
                (g_im * x_re - g_re * x_im) * inv_root,
            ],
            axis=1,
        )
        product = jnp.concatenate([real, imag], axis=0).astype(jnp.bfloat16)
        back = jnp.dot(inner_back_ref[...], product, preferred_element_type=jnp.float32)
        cos = jnp.concatenate([cos_ref[k]] * 3, axis=1)
        sin = jnp.concatenate([sin_ref[k]] * 3, axis=1)
        work[k, :S, :] = (back[:S] * cos - back[S:] * sin).astype(jnp.bfloat16)
        work[k, S:, :] = (back[S:] * cos + back[:S] * sin).astype(jnp.bfloat16)

    batch = next(n for n in (3, 5, 1) if k_count % n == 0)

    def some_rows(step, carry):
        for i in range(batch):
            one_row(step * batch + i)
        return carry

    lax.fori_loop(0, k_count // batch, some_rows, 0)

    def last_section(step, carry):
        at = pl.multiple_of(step * G, G)
        pieces = [work[k, pl.ds(at, G), :] for k in range(k_count)]
        pieces += [work[k, pl.ds(S + at, G), :] for k in range(1, half_rows)]
        signal = jnp.dot(
            back_ref[...], jnp.concatenate(pieces, axis=0), preferred_element_type=jnp.float32
        )
        signal = (signal * scale).astype(jnp.bfloat16)
        for r in range(half_rows):
            rows = pl.ds((r % rows_per) * S + at, G)
            part = signal[r * G : (r + 1) * G]
            cg_ref[r // rows_per, 0, rows, :] = part[:, :LANES]
            cg_ref[r // rows_per, 1, rows, :] = part[:, LANES : 2 * LANES]
            gf_ref[r // rows_per, rows, :] = part[:, 2 * LANES :]
        return carry

    lax.fori_loop(0, S // G, last_section, 0)


def transform_chunk(xg, tables, inv_root, scale):
    k_count = tables[4].shape[0]
    lanes = xg.shape[-1]
    if lanes < LANES:
        xg = jnp.pad(xg, ((0, 0),) * 3 + ((0, LANES - lanes),))
    cg, gf = pl.pallas_call(
        functools.partial(spectral_kernel, inv_root, scale),
        out_shape=(
            jax.ShapeDtypeStruct((xg.shape[0], 2) + xg.shape[2:], jnp.bfloat16),
            jax.ShapeDtypeStruct(xg.shape[:1] + xg.shape[2:], jnp.bfloat16),
        ),
        in_specs=[pl.BlockSpec(memory_space=pltpu.VMEM)] * 7,
        out_specs=(pl.BlockSpec(memory_space=pltpu.VMEM),) * 2,
        scratch_shapes=[pltpu.VMEM((k_count, 2 * S, 3 * LANES), jnp.bfloat16)],
        compiler_params=pltpu.CompilerParams(vmem_limit_bytes=58 * 1024 * 1024),
        cost_estimate=pl.CostEstimate(
            flops=13_000_000_000, bytes_accessed=16_000_000, transcendentals=0
        ),
    )(xg, *tables)
    return cg[..., :lanes], gf[..., :lanes]


def later(x, head):
    row = lax.broadcasted_iota(jnp.int32, x.shape, 0)
    one = jnp.where(row == 0, head[1:2], pltpu.roll(x, 1, 0))
    two = jnp.where(row == 0, head[0:1], jnp.where(row == 1, head[1:2], pltpu.roll(x, 2, 0)))
    return (x, one, two)


def sooner(x, tail):
    count = x.shape[0]
    row = lax.broadcasted_iota(jnp.int32, x.shape, 0)
    one = jnp.where(row == count - 1, tail[0:1], pltpu.roll(x, count - 1, 0))
    two = jnp.where(
        row == count - 1,
        tail[1:2],
        jnp.where(row == count - 2, tail[0:1], pltpu.roll(x, count - 2, 0)),
    )
    return (x, one, two)


def weigh(shifted, weights):
    return sum(weights[j : j + 1] * shifted[j] for j in range(len(shifted)))


def as_float(ref):
    return ref[...].astype(jnp.float32)


def rounded(x):
    return x.astype(jnp.bfloat16)


def unpack_kernel(gf_ref, out_ref):
    per, chunks, _, lanes = gf_ref.shape
    for i in range(per):
        for c in range(chunks):
            at = (i * chunks + c) * lanes
            out_ref[:, at : at + lanes] = gf_ref[i, c]


def entry_kernel(q_ref, k_ref, v_ref, cot_ref, ahead_ref, w_ref, h_ref, *outs):
    ahead = as_float(ahead_ref)
    per, _, _, lanes = outs[0].shape
    shorts = []
    for i, ref in enumerate((q_ref, k_ref, v_ref)):
        shorts.append(weigh(later(as_float(ref), ahead[2 * i : 2 * i + 2]), w_ref[i]))
    mixed = rounded(shorts[1] * shorts[2])
    grad_conv = rounded(as_float(cot_ref) * shorts[0])
    for i in range(per):
        for c, out in enumerate(outs):
            at = (i * len(outs) + c) * lanes
            out[i, 0] = mixed[:, at : at + lanes]
            out[i, 1] = grad_conv[:, at : at + lanes]
            out[i, 2] = h_ref[:, at : at + lanes]


def local_grads(q_ref, k_ref, v_ref, cot_ref, ahead_ref, w_ref, conv, grad_mixed):
    ahead = as_float(ahead_ref)
    shifted = []
    shorts = []
    for i, ref in enumerate((q_ref, k_ref, v_ref)):
        shifted.append(later(as_float(ref), ahead[2 * i : 2 * i + 2]))
        shorts.append(weigh(shifted[i], w_ref[i]))
    grads = [as_float(cot_ref) * conv, grad_mixed * shorts[2], grad_mixed * shorts[1]]
    grads = [rounded(g).astype(jnp.float32) for g in grads]
    return shifted, shorts, grads


def gather_lanes(cg_refs, which, blocks):
    parts = [cg[i, which] for i in blocks for cg in cg_refs]
    return jnp.concatenate(parts, axis=1).astype(jnp.float32)


def edge_kernel(q_ref, k_ref, v_ref, cot_ref, ahead_ref, w_ref, *rest):
    cg_refs, edge_ref = rest[:-1], rest[-1]
    blocks = range(cg_refs[0].shape[0])
    conv = gather_lanes(cg_refs, 0, blocks)
    grad_mixed = gather_lanes(cg_refs, 1, blocks)
    _, _, grads = local_grads(
        q_ref, k_ref, v_ref, cot_ref, ahead_ref, w_ref, conv, grad_mixed
    )
    for i in range(3):
        edge_ref[2 * i : 2 * i + 2, :] = rounded(grads[i][:2])


def exit_kernel(chunks, q_ref, k_ref, v_ref, cot_ref, ahead_ref, w_ref, behind_ref, *rest):
    cg_refs = rest[:chunks]
    out_ref, gq_ref, gk_ref, gv_ref, short_ref = rest[chunks:]
    blocks = range(cg_refs[0].shape[0])
    conv = gather_lanes(cg_refs, 0, blocks)
    grad_mixed = gather_lanes(cg_refs, 1, blocks)
    shifted, shorts, grads = local_grads(
        q_ref, k_ref, v_ref, cot_ref, ahead_ref, w_ref, conv, grad_mixed
    )
    out_ref[...] = rounded(shorts[0] * conv)
    behind = as_float(behind_ref)
    for i, ref in enumerate((gq_ref, gk_ref, gv_ref)):
        ref[...] = rounded(weigh(sooner(grads[i], behind[2 * i : 2 * i + 2]), w_ref[i]))
        for j in range(3):
            short_ref[i, j : j + 1, :] = jnp.sum(grads[i] * shifted[i][j], axis=0, keepdims=True)


def exchange(x):
    return lax.all_to_all(x, "ctx", split_axis=0, concat_axis=0, tiled=True)


def sum_over(x, axis):
    count = lax.axis_size(axis)

    def partner(y, flip):
        return lax.ppermute(y, axis, [(i, i ^ flip) for i in range(count)])

    step = 1
    while step < count:
        if 2 * step < count:
            x = (x + partner(x, step)) + (partner(x, 2 * step) + partner(x, 3 * step))
            step *= 4
        else:
            x = x + partner(x, step)
            step *= 2
    return x


def on_device(query_in, key_in, value_in, cotangent, short_weight, long_filter):
    local_rows, channels = query_in.shape
    tap_count = short_weight.shape[1]
    rim_rows = tap_count - 1
    ctx_size = lax.axis_size("ctx")
    length = local_rows * ctx_size
    fft_size = 2 * length
    outer_len = fft_size // S
    inv_root = 1.0 / math.sqrt(length)
    own = channels // ctx_size
    lanes = min(own, LANES)
    chunks = own // lanes
    width = max(own, LANES)
    per = width // own
    steps = channels // width
    limit = pltpu.CompilerParams(vmem_limit_bytes=58 * 1024 * 1024)
    stream = pl.BlockSpec((local_rows, width), lambda i: (0, i))
    rim = pl.BlockSpec((3 * rim_rows, width), lambda i: (0, i))
    taps = pl.BlockSpec((3, tap_count, width), lambda i: (0, 0, i))
    pair = pl.BlockSpec((per, 2, local_rows, lanes), lambda i: (i, 0, 0, 0))
    triple = pl.BlockSpec((per, 3, local_rows, lanes), lambda i: (i, 0, 0, 0))
    packed = pl.BlockSpec((per, chunks, local_rows, lanes), lambda i: (i, 0, 0, 0))
    whole = jax.ShapeDtypeStruct((local_rows, channels), jnp.bfloat16)

    first, back, inner_fwd, inner_back, turn_cos, turn_sin = grid_tables(outer_len)
    tables = (
        spread_over_rows(first),
        spread_over_rows(back),
        jnp.asarray(inner_fwd, jnp.bfloat16),
        jnp.asarray(inner_back, jnp.bfloat16),
        jnp.broadcast_to(
            jnp.asarray(turn_cos, jnp.float32)[:, :, None], turn_cos.shape + (LANES,)
        ),
        jnp.broadcast_to(
            jnp.asarray(turn_sin, jnp.float32)[:, :, None], turn_sin.shape + (LANES,)
        ),
    )
    tails = jnp.concatenate([x[local_rows - rim_rows :] for x in (query_in, key_in, value_in)])
    ahead = from_behind(tails, "ctx", 1)
    streams = (query_in, key_in, value_in, cotangent, ahead, short_weight)
    xg_parts = pl.pallas_call(
        entry_kernel,
        grid=(steps,),
        out_shape=(
            jax.ShapeDtypeStruct((ctx_size, 3, local_rows, lanes), jnp.bfloat16),
        )
        * chunks,
        in_specs=[stream] * 4 + [rim, taps, stream],
        out_specs=(triple,) * chunks,
        compiler_params=limit,
        cost_estimate=pl.CostEstimate(
            flops=100_000_000, bytes_accessed=12_000_000, transcendentals=0
        ),
    )(*streams, long_filter)
    xg_parts = [exchange(xg) for xg in xg_parts]
    cg_parts, gf_parts = [], []
    for xg in xg_parts:
        cg, gf = transform_chunk(xg, tables, inv_root, 1.0 / fft_size)
        cg_parts.append(exchange(cg))
        gf_parts.append(gf)
    gf_back = exchange(jnp.stack(gf_parts, axis=1))
    top = pl.BlockSpec((G, channels), lambda i: (0, 0))
    edge = pl.pallas_call(
        edge_kernel,
        grid=(1,),
        out_shape=jax.ShapeDtypeStruct((3 * rim_rows, channels), jnp.bfloat16),
        in_specs=[top] * 4
        + [
            pl.BlockSpec((3 * rim_rows, channels), lambda i: (0, 0)),
            pl.BlockSpec((3, tap_count, channels), lambda i: (0, 0, 0)),
        ]
        + [pl.BlockSpec((ctx_size, 2, G, lanes), lambda i: (0, 0, 0, 0))] * chunks,
        out_specs=pl.BlockSpec((3 * rim_rows, channels), lambda i: (0, 0)),
        compiler_params=limit,
    )(*streams, *cg_parts)
    behind = from_behind(edge, "ctx", -1)
    block_out, grad_query, grad_key, grad_value, short_part = pl.pallas_call(
        functools.partial(exit_kernel, chunks),
        grid=(steps,),
        out_shape=(whole,) * 4 + (jax.ShapeDtypeStruct((3, tap_count, channels), jnp.float32),),
        in_specs=[stream] * 4 + [rim, taps, rim] + [pair] * chunks,
        out_specs=(stream,) * 4 + (taps,),
        compiler_params=limit,
        cost_estimate=pl.CostEstimate(
            flops=200_000_000, bytes_accessed=20_000_000, transcendentals=0
        ),
    )(*streams, behind, *cg_parts)
    short_part, gf_back = lax.optimization_barrier((short_part, gf_back))
    grad_short = sum_over(short_part, "ctx") * inv_root
    grad_filter = pl.pallas_call(
        unpack_kernel,
        grid=(steps,),
        out_shape=whole,
        in_specs=[packed],
        out_specs=stream,
        compiler_params=limit,
    )(gf_back)
    return (block_out, grad_query, grad_key, grad_value, grad_short, grad_filter)


def solution(mesh):
    in_specs = (
        P("ctx", "tp"),
        P("ctx", "tp"),
        P("ctx", "tp"),
        P("ctx", "tp"),
        P(None, None, "tp"),
        P("ctx", "tp"),
    )
    out_specs = (
        P("ctx", "tp"),
        P("ctx", "tp"),
        P("ctx", "tp"),
        P("ctx", "tp"),
        P(None, None, "tp"),
        P("ctx", "tp"),
    )
    return jax.shard_map(
        on_device, mesh=mesh, in_specs=in_specs, out_specs=out_specs, check_vma=False
    )
```

```python
import functools
import math

import jax
import jax.numpy as jnp
import numpy as np
from jax import lax
from jax.experimental import pallas as pl
from jax.experimental.pallas import tpu as pltpu
from jax.sharding import PartitionSpec as P

S = 128
G = 16
LANES = 128


def from_behind(x, axis, by):
    count = lax.axis_size(axis)
    pairs = [(i, i + by) for i in range(count) if 0 <= i + by < count]
    return lax.ppermute(x, axis, pairs)


def grid_tables(outer_len):
    half_rows = outer_len // 2
    k_count = half_rows + 1
    k_ids = np.arange(k_count)[:, None]
    r_ids = np.arange(half_rows)[None, :]
    angle = 2.0 * np.pi / outer_len * (k_ids * r_ids % outer_len)
    first = np.concatenate([np.cos(angle), -np.sin(angle)[1:half_rows]], axis=0)
    weight = np.full((k_count, 1), 2.0)
    weight[0] = weight[half_rows] = 1.0
    back = np.concatenate([weight * np.cos(angle), -2.0 * np.sin(angle)[1:half_rows]], axis=0).T
    inner = 2.0 * np.pi / S * (np.arange(S)[:, None] * np.arange(S)[None, :] % S)
    cos, sin = np.cos(inner), np.sin(inner)
    inner_fwd = np.block([[cos, sin], [-sin, cos]])
    inner_back = np.block([[cos, -sin], [sin, cos]])
    turn = 2.0 * np.pi / (outer_len * S) * (k_ids * np.arange(S)[None, :])
    return first, back, inner_fwd, inner_back, np.cos(turn), np.sin(turn)


def spread_over_rows(table):
    return jnp.asarray(np.kron(table, np.eye(G)).astype(jnp.bfloat16))


def spectral_kernel(
    inv_root,
    scale,
    xg_ref,
    first_ref,
    back_ref,
    inner_fwd_ref,
    inner_back_ref,
    cos_ref,
    sin_ref,
    cg_ref,
    gf_ref,
    work,
):
    k_count = work.shape[0]
    half_rows = k_count - 1
    rows_per = xg_ref.shape[2] // S

    def first_section(step, carry):
        at = pl.multiple_of(step * G, G)
        pieces = []
        for r in range(half_rows):
            rows = pl.ds((r % rows_per) * S + at, G)
            pieces.append(
                jnp.concatenate(
                    [
                        xg_ref[r // rows_per, 0, rows, :],
                        xg_ref[r // rows_per, 1, rows, :],
                        xg_ref[r // rows_per, 2, rows, :],
                    ],
                    axis=1,
                )
            )
        grid_rows = jnp.concatenate(pieces, axis=0)
        first = jnp.dot(first_ref[...], grid_rows, preferred_element_type=jnp.float32)
        for k in range(k_count):
            re = first[k * G : (k + 1) * G]
            cos = jnp.concatenate([cos_ref[k, pl.ds(at, G), :]] * 3, axis=1)
            sin = jnp.concatenate([sin_ref[k, pl.ds(at, G), :]] * 3, axis=1)
            if 0 < k < half_rows:
                row = (k_count + k - 1) * G
                im = first[row : row + G]
                turned_re = re * cos + im * sin
                turned_im = im * cos - re * sin
            else:
                turned_re = re * cos
                turned_im = -re * sin
            work[k, pl.ds(at, G), :] = turned_re.astype(jnp.bfloat16)
            work[k, pl.ds(S + at, G), :] = turned_im.astype(jnp.bfloat16)
        return carry

    lax.fori_loop(0, S // G, first_section, 0)

    def one_row(k):
        spec = jnp.dot(inner_fwd_ref[...], work[k], preferred_element_type=jnp.float32)
        spec = spec.astype(jnp.bfloat16).astype(jnp.float32)
        x_re, x_im = spec[:S, :LANES], spec[S:, :LANES]
        g_re, g_im = spec[:S, LANES : 2 * LANES], spec[S:, LANES : 2 * LANES]
        h_re, h_im = spec[:S, 2 * LANES :], spec[S:, 2 * LANES :]
        real = jnp.concatenate(
            [
                x_re * h_re - x_im * h_im,
                g_re * h_re + g_im * h_im,
                (g_re * x_re + g_im * x_im) * inv_root,
            ],
            axis=1,
        )
        imag = jnp.concatenate(
            [
                x_re * h_im + x_im * h_re,
                g_im * h_re - g_re * h_im,
                (g_im * x_re - g_re * x_im) * inv_root,
            ],
            axis=1,
        )
        product = jnp.concatenate([real, imag], axis=0).astype(jnp.bfloat16)
        back = jnp.dot(inner_back_ref[...], product, preferred_element_type=jnp.float32)
        cos = jnp.concatenate([cos_ref[k]] * 3, axis=1)
        sin = jnp.concatenate([sin_ref[k]] * 3, axis=1)
        work[k, :S, :] = (back[:S] * cos - back[S:] * sin).astype(jnp.bfloat16)
        work[k, S:, :] = (back[S:] * cos + back[:S] * sin).astype(jnp.bfloat16)

    batch = next(n for n in (3, 5, 1) if k_count % n == 0)

    def some_rows(step, carry):
        for i in range(batch):
            one_row(step * batch + i)
        return carry

    lax.fori_loop(0, k_count // batch, some_rows, 0)

    def last_section(step, carry):
        at = pl.multiple_of(step * G, G)
        pieces = [work[k, pl.ds(at, G), :] for k in range(k_count)]
        pieces += [work[k, pl.ds(S + at, G), :] for k in range(1, half_rows)]
        signal = jnp.dot(
            back_ref[...], jnp.concatenate(pieces, axis=0), preferred_element_type=jnp.float32
        )
        signal = (signal * scale).astype(jnp.bfloat16)
        for r in range(half_rows):
            rows = pl.ds((r % rows_per) * S + at, G)
            part = signal[r * G : (r + 1) * G]
            cg_ref[r // rows_per, 0, rows, :] = part[:, :LANES]
            cg_ref[r // rows_per, 1, rows, :] = part[:, LANES : 2 * LANES]
            gf_ref[r // rows_per, rows, :] = part[:, 2 * LANES :]
        return carry

    lax.fori_loop(0, S // G, last_section, 0)


def transform_chunk(xg, tables, inv_root, scale):
    k_count = tables[4].shape[0]
    lanes = xg.shape[-1]
    if lanes < LANES:
        xg = jnp.pad(xg, ((0, 0),) * 3 + ((0, LANES - lanes),))
    cg, gf = pl.pallas_call(
        functools.partial(spectral_kernel, inv_root, scale),
        out_shape=(
            jax.ShapeDtypeStruct((xg.shape[0], 2) + xg.shape[2:], jnp.bfloat16),
            jax.ShapeDtypeStruct(xg.shape[:1] + xg.shape[2:], jnp.bfloat16),
        ),
        in_specs=[pl.BlockSpec(memory_space=pltpu.VMEM)] * 7,
        out_specs=(pl.BlockSpec(memory_space=pltpu.VMEM),) * 2,
        scratch_shapes=[pltpu.VMEM((k_count, 2 * S, 3 * LANES), jnp.bfloat16)],
        compiler_params=pltpu.CompilerParams(vmem_limit_bytes=58 * 1024 * 1024),
        cost_estimate=pl.CostEstimate(
            flops=13_000_000_000, bytes_accessed=16_000_000, transcendentals=0
        ),
    )(xg, *tables)
    return cg[..., :lanes], gf[..., :lanes]


def later(x, head):
    row = lax.broadcasted_iota(jnp.int32, x.shape, 0)
    one = jnp.where(row == 0, head[1:2], pltpu.roll(x, 1, 0))
    two = jnp.where(row == 0, head[0:1], jnp.where(row == 1, head[1:2], pltpu.roll(x, 2, 0)))
    return (x, one, two)


def sooner(x, tail):
    count = x.shape[0]
    row = lax.broadcasted_iota(jnp.int32, x.shape, 0)
    one = jnp.where(row == count - 1, tail[0:1], pltpu.roll(x, count - 1, 0))
    two = jnp.where(
        row == count - 1,
        tail[1:2],
        jnp.where(row == count - 2, tail[0:1], pltpu.roll(x, count - 2, 0)),
    )
    return (x, one, two)


def weigh(shifted, weights):
    return sum(weights[j : j + 1] * shifted[j] for j in range(len(shifted)))


def as_float(ref):
    return ref[...].astype(jnp.float32)


def rounded(x):
    return x.astype(jnp.bfloat16)


def unpack_kernel(gf_ref, out_ref):
    per, chunks, _, lanes = gf_ref.shape
    for i in range(per):
        for c in range(chunks):
            at = (i * chunks + c) * lanes
            out_ref[:, at : at + lanes] = gf_ref[i, c]


def entry_kernel(q_ref, k_ref, v_ref, cot_ref, ahead_ref, w_ref, h_ref, *outs):
    ahead = as_float(ahead_ref)
    per, _, _, lanes = outs[0].shape
    shorts = []
    for i, ref in enumerate((q_ref, k_ref, v_ref)):
        shorts.append(weigh(later(as_float(ref), ahead[2 * i : 2 * i + 2]), w_ref[i]))
    mixed = rounded(shorts[1] * shorts[2])
    grad_conv = rounded(as_float(cot_ref) * shorts[0])
    for i in range(per):
        for c, out in enumerate(outs):
            at = (i * len(outs) + c) * lanes
            out[i, 0] = mixed[:, at : at + lanes]
            out[i, 1] = grad_conv[:, at : at + lanes]
            out[i, 2] = h_ref[:, at : at + lanes]


def local_grads(q_ref, k_ref, v_ref, cot_ref, ahead_ref, w_ref, conv, grad_mixed):
    ahead = as_float(ahead_ref)
    shifted = []
    shorts = []
    for i, ref in enumerate((q_ref, k_ref, v_ref)):
        shifted.append(later(as_float(ref), ahead[2 * i : 2 * i + 2]))
        shorts.append(weigh(shifted[i], w_ref[i]))
    grads = [as_float(cot_ref) * conv, grad_mixed * shorts[2], grad_mixed * shorts[1]]
    grads = [rounded(g).astype(jnp.float32) for g in grads]
    return shifted, shorts, grads


def gather_lanes(cg_refs, which, blocks):
    parts = [cg[i, which] for i in blocks for cg in cg_refs]
    return jnp.concatenate(parts, axis=1).astype(jnp.float32)


def edge_kernel(q_ref, k_ref, v_ref, cot_ref, ahead_ref, w_ref, *rest):
    cg_refs, edge_ref = rest[:-1], rest[-1]
    blocks = range(cg_refs[0].shape[0])
    conv = gather_lanes(cg_refs, 0, blocks)
    grad_mixed = gather_lanes(cg_refs, 1, blocks)
    _, _, grads = local_grads(
        q_ref, k_ref, v_ref, cot_ref, ahead_ref, w_ref, conv, grad_mixed
    )
    for i in range(3):
        edge_ref[2 * i : 2 * i + 2, :] = rounded(grads[i][:2])


def exit_kernel(chunks, q_ref, k_ref, v_ref, cot_ref, ahead_ref, w_ref, behind_ref, *rest):
    cg_refs = rest[:chunks]
    out_ref, gq_ref, gk_ref, gv_ref, short_ref = rest[chunks:]
    blocks = range(cg_refs[0].shape[0])
    conv = gather_lanes(cg_refs, 0, blocks)
    grad_mixed = gather_lanes(cg_refs, 1, blocks)
    shifted, shorts, grads = local_grads(
        q_ref, k_ref, v_ref, cot_ref, ahead_ref, w_ref, conv, grad_mixed
    )
    out_ref[...] = rounded(shorts[0] * conv)
    behind = as_float(behind_ref)
    for i, ref in enumerate((gq_ref, gk_ref, gv_ref)):
        ref[...] = rounded(weigh(sooner(grads[i], behind[2 * i : 2 * i + 2]), w_ref[i]))
        for j in range(3):
            short_ref[i, j : j + 1, :] = jnp.sum(grads[i] * shifted[i][j], axis=0, keepdims=True)


def exchange(x):
    return lax.all_to_all(x, "ctx", split_axis=0, concat_axis=0, tiled=True)


def sum_over(x):
    rows, channels = x.shape
    count = lax.axis_size("ctx")
    terms = exchange(x.reshape(rows, count, channels // count).transpose(1, 0, 2))
    total = jnp.sum(terms, axis=0)
    totals = exchange(jnp.broadcast_to(total[None], terms.shape))
    return totals.transpose(1, 0, 2).reshape(rows, channels)


def on_device(query_in, key_in, value_in, cotangent, short_weight, long_filter):
    local_rows, channels = query_in.shape
    tap_count = short_weight.shape[1]
    rim_rows = tap_count - 1
    ctx_size = lax.axis_size("ctx")
    length = local_rows * ctx_size
    fft_size = 2 * length
    outer_len = fft_size // S
    inv_root = 1.0 / math.sqrt(length)
    own = channels // ctx_size
    lanes = min(own, LANES)
    chunks = own // lanes
    width = max(own, LANES)
    per = width // own
    steps = channels // width
    limit = pltpu.CompilerParams(vmem_limit_bytes=58 * 1024 * 1024)
    stream = pl.BlockSpec((local_rows, width), lambda i: (0, i))
    rim = pl.BlockSpec((3 * rim_rows, width), lambda i: (0, i))
    taps = pl.BlockSpec((3, tap_count, width), lambda i: (0, 0, i))
    pair = pl.BlockSpec((per, 2, local_rows, lanes), lambda i: (i, 0, 0, 0))
    triple = pl.BlockSpec((per, 3, local_rows, lanes), lambda i: (i, 0, 0, 0))
    packed = pl.BlockSpec((per, chunks, local_rows, lanes), lambda i: (i, 0, 0, 0))
    whole = jax.ShapeDtypeStruct((local_rows, channels), jnp.bfloat16)

    first, back, inner_fwd, inner_back, turn_cos, turn_sin = grid_tables(outer_len)
    tables = (
        spread_over_rows(first),
        spread_over_rows(back),
        jnp.asarray(inner_fwd, jnp.bfloat16),
        jnp.asarray(inner_back, jnp.bfloat16),
        jnp.broadcast_to(
            jnp.asarray(turn_cos, jnp.float32)[:, :, None], turn_cos.shape + (LANES,)
        ),
        jnp.broadcast_to(
            jnp.asarray(turn_sin, jnp.float32)[:, :, None], turn_sin.shape + (LANES,)
        ),
    )
    tails = jnp.concatenate([x[local_rows - rim_rows :] for x in (query_in, key_in, value_in)])
    ahead = from_behind(tails, "ctx", 1)
    streams = (query_in, key_in, value_in, cotangent, ahead, short_weight)
    xg_parts = pl.pallas_call(
        entry_kernel,
        grid=(steps,),
        out_shape=(
            jax.ShapeDtypeStruct((ctx_size, 3, local_rows, lanes), jnp.bfloat16),
        )
        * chunks,
        in_specs=[stream] * 4 + [rim, taps, stream],
        out_specs=(triple,) * chunks,
        compiler_params=limit,
        cost_estimate=pl.CostEstimate(
            flops=100_000_000, bytes_accessed=12_000_000, transcendentals=0
        ),
    )(*streams, long_filter)
    xg_parts = [exchange(xg) for xg in xg_parts]
    cg_parts, gf_parts = [], []
    for xg in xg_parts:
        cg, gf = transform_chunk(xg, tables, inv_root, 1.0 / fft_size)
        cg_parts.append(exchange(cg))
        gf_parts.append(gf)
    gf_back = exchange(jnp.stack(gf_parts, axis=1))
    top = pl.BlockSpec((G, channels), lambda i: (0, 0))
    edge = pl.pallas_call(
        edge_kernel,
        grid=(1,),
        out_shape=jax.ShapeDtypeStruct((3 * rim_rows, channels), jnp.bfloat16),
        in_specs=[top] * 4
        + [
            pl.BlockSpec((3 * rim_rows, channels), lambda i: (0, 0)),
            pl.BlockSpec((3, tap_count, channels), lambda i: (0, 0, 0)),
        ]
        + [pl.BlockSpec((ctx_size, 2, G, lanes), lambda i: (0, 0, 0, 0))] * chunks,
        out_specs=pl.BlockSpec((3 * rim_rows, channels), lambda i: (0, 0)),
        compiler_params=limit,
    )(*streams, *cg_parts)
    behind = from_behind(edge, "ctx", -1)
    block_out, grad_query, grad_key, grad_value, short_part = pl.pallas_call(
        functools.partial(exit_kernel, chunks),
        grid=(steps,),
        out_shape=(whole,) * 4 + (jax.ShapeDtypeStruct((3, tap_count, channels), jnp.float32),),
        in_specs=[stream] * 4 + [rim, taps, rim] + [pair] * chunks,
        out_specs=(stream,) * 4 + (taps,),
        compiler_params=limit,
        cost_estimate=pl.CostEstimate(
            flops=200_000_000, bytes_accessed=20_000_000, transcendentals=0
        ),
    )(*streams, behind, *cg_parts)
    short_total = sum_over(short_part.reshape(3 * tap_count, channels))
    grad_short = short_total.reshape(3, tap_count, channels) * inv_root
    grad_filter = pl.pallas_call(
        unpack_kernel,
        grid=(steps,),
        out_shape=whole,
        in_specs=[packed],
        out_specs=stream,
        compiler_params=limit,
    )(gf_back)
    return (block_out, grad_query, grad_key, grad_value, grad_short, grad_filter)


def solution(mesh):
    in_specs = (
        P("ctx", "tp"),
        P("ctx", "tp"),
        P("ctx", "tp"),
        P("ctx", "tp"),
        P(None, None, "tp"),
        P("ctx", "tp"),
    )
    out_specs = (
        P("ctx", "tp"),
        P("ctx", "tp"),
        P("ctx", "tp"),
        P("ctx", "tp"),
        P(None, None, "tp"),
        P("ctx", "tp"),
    )
    return jax.shard_map(
        on_device, mesh=mesh, in_specs=in_specs, out_specs=out_specs, check_vma=False
    )
```
